32 devices in a mesh: groups: 2 (over x), owners: 16 (over z, y, core).
Axes of the slice: x: 2, y: 2, z: 4, core: 2. Of those that a mesh axis runs over, the one named last changes fastest.
Arguments:
- embeddings: bfloat16 [65536, 1536], P(('groups', 'owners')), parts along dimension 0, may hold values from -40 to 40
- level_ids: int32 [65536], P(('groups', 'owners')), parts along dimension 0, may hold values from 0 to 63, as said below
- centroids: float32 [2048, 1536], P(('groups', 'owners')), parts along dimension 0, may hold values from -8 to 8
- empty_ids: int32 [32], P('groups'), parts along dimension 0, may hold values from 0 to 1023, as said below
- reseed_rows: int32 [32], P('groups'), parts along dimension 0, may hold values from 0 to 32767
Outputs:
- new_centroids: float32 [2048, 1536], P(('groups', 'owners')), parts along dimension 0
- counts: float32 [2048], P(('groups', 'owners')), parts along dimension 0
The draws below stay inside these ranges and needn't reach their ends.
There are 2 independent parts, one for each index of `groups`. The reference program is written for one: setup_inputs(seed, part) draws one part's arguments, and reference() takes and returns one part's arrays. A program takes and returns all parts, laid end to end along the dimension named above; each array names one. Nothing has to cross between parts.
Inputs may be any that keep to these rules, and one draw needn't show every extreme that they name: `level_ids`: row i lies on owner i // 2048; the level-1 cluster (K / (16 × 4); 8 on the larger slice) l is held by owner l // 4. From the rows of one owner at most 256 go to any one owner; in every draw some owner receives exactly 256 rows from every owner. `empty_ids`: the ids are distinct.
All inputs are finite; a program needn't handle non-finite values.
Results may differ from the reference program's by a relative error of at most 0.0075.
Values may be sent and summed in bfloat16 or wider, within the bound.
A program may use at most 128 MiB of HBM per device.

```python
import math
import jax
import jax.numpy as jnp
from jax import lax

D = 1536
K = 1024
ROWS = 2048
L1_DEV = 4
EMPTY = 16
TOKENS = 32768
SUB = 16
N_OWNERS = 16


def level_helper(key):
    key = jax.random.fold_in(key, 101)
    owner_count = N_OWNERS
    row_count = ROWS
    hot_key, score_key, perm_key, choice_key = jax.random.split(key, 4)
    hot_owner = jax.random.randint(hot_key, (), 0, owner_count)
    scores = jax.random.randint(score_key, (owner_count, owner_count), 0, 1 << 20)
    scores = scores * owner_count + jnp.arange(owner_count)[None, :]
    scores = jnp.where(jnp.arange(owner_count)[None, :] == hot_owner, -1, scores)
    ranked = jnp.argsort(scores, axis=1, stable=True)
    quarter = owner_count // 4
    rank_ids = jnp.arange(owner_count)
    mean_load = row_count // owner_count
    per_rank = jnp.where(rank_ids < quarter, 2 * mean_load, jnp.where(rank_ids < 3 * quarter, mean_load, 0))
    bounds = jnp.cumsum(per_rank)
    slot_rank = jnp.sum(jnp.arange(row_count)[:, None] >= bounds[None, :], axis=1)
    slot_owner = ranked[:, slot_rank]
    perm_keys = jax.random.split(perm_key, owner_count)

    def shuffle_one(one_key, values):
        return jax.random.permutation(one_key, values)
    shuffled = jax.vmap(shuffle_one)(perm_keys, slot_owner)
    sub_ids = jax.random.randint(choice_key, (owner_count, row_count), 0, L1_DEV)
    return (shuffled * L1_DEV + sub_ids).reshape(-1).astype(jnp.int32)


def centroid_helper(key):
    base = jax.random.truncated_normal(jax.random.fold_in(key, 202), -6.0, 6.0, (K, D), jnp.float32)
    noise = jax.random.truncated_normal(jax.random.fold_in(key, 203), -6.0, 6.0, (K, D), jnp.float32)
    paired = (jnp.arange(K) % SUB == 1)[:, None]
    return jnp.where(paired, noise, base)


def draw_level_ids(key, part):
    return level_helper(key)


def draw_centroids(key, part):
    return centroid_helper(key)


def draw_embeddings(key, part):
    base_key = jax.random.fold_in(key, 303)
    drawn = jax.random.truncated_normal(base_key, -6.0, 6.0, (TOKENS, D), jnp.float32)
    return drawn.astype(jnp.bfloat16)


def draw_empty_ids(key, part):
    key = jax.random.fold_in(key, 404)
    return jax.random.permutation(key, K)[:EMPTY].astype(jnp.int32)


def place_ends(array, own_key, low, high):
    longest = array.shape.index(max(array.shape))
    spots = []
    for shift in (0, 1):
        where = [jax.random.randint(jax.random.fold_in(own_key, axis), (), 0, length) for axis, length in enumerate(array.shape)]
        where[longest] = (where[longest] + shift) % array.shape[longest]
        spots.append(tuple(where))
    return array.at[spots[0]].set(low).at[spots[1]].set(high)


def setup_inputs(seed: int = 0, part: int = 0) -> dict:
    arg_keys = jax.random.split(jax.random.key(seed), 6)
    part_splits = jax.random.split(jax.random.fold_in(arg_keys[5], part), 6)
    return {
        "embeddings": draw_embeddings(jax.random.fold_in(jax.random.fold_in(arg_keys[5], part), 71), part),
        "level_ids": draw_level_ids(jax.random.fold_in(jax.random.fold_in(arg_keys[5], part), 71), part),
        "centroids": draw_centroids(jax.random.fold_in(jax.random.fold_in(arg_keys[5], part), 71), part),
        "empty_ids": draw_empty_ids(jax.random.fold_in(jax.random.fold_in(arg_keys[5], part), 71), part),
        "reseed_rows": place_ends(jax.random.randint(part_splits[4], (EMPTY,), 0, TOKENS), jax.random.fold_in(part_splits[4], 1), 0, TOKENS - 1).astype(jnp.int32),
    }


PRIOR = 8.0

def reference(embeddings, level_ids, centroids, empty_ids, reseed_rows):
    centroid_b = centroids.astype(jnp.bfloat16)
    centroid_wide = lax.optimization_barrier(centroid_b).astype(jnp.float32)
    norms_sq = lax.optimization_barrier(jnp.sum(centroid_wide * centroid_wide, axis=1))
    block = min(1024, TOKENS)
    offsets = jnp.arange(SUB, dtype=jnp.int32)

    def step_fn(carry, pieces):
        totals, counts = carry
        block_rows, block_ids = pieces
        member_ids = (block_ids[:, None] * SUB + offsets[None, :]).astype(jnp.int32)
        gathered = centroid_wide[member_ids]
        wide_rows = block_rows.astype(jnp.float32)
        products = jnp.einsum('bd,bsd->bs', wide_rows, gathered, precision=lax.Precision.HIGHEST)
        logits = (products - 0.5 * norms_sq[member_ids]) / math.sqrt(D)
        weights = jax.nn.softmax(logits, axis=-1)
        weights_b = lax.optimization_barrier(weights.astype(jnp.bfloat16)).astype(jnp.float32)
        terms = weights_b[:, :, None] * wide_rows[:, None, :]
        flat_ids = member_ids.reshape(-1)
        totals = totals.at[flat_ids].add(terms.reshape(-1, D))
        counts = counts.at[flat_ids].add(weights.reshape(-1))
        return ((totals, counts), None)
    start = (jnp.zeros((K, D), jnp.float32), jnp.zeros((K,), jnp.float32))
    (totals, counts), _ = lax.scan(step_fn, start, (embeddings.reshape(-1, block, D), level_ids.reshape(-1, block)))
    updated = (totals + PRIOR * centroids) / (counts + PRIOR)[:, None]
    reseeded = embeddings[reseed_rows].astype(jnp.float32)
    new_centroids = updated.at[empty_ids].set(reseeded)
    return (new_centroids, counts)
```

```python
import functools
import math

import jax
import jax.numpy as jnp
from jax import lax
from jax.experimental import pallas as pl
from jax.experimental.pallas import tpu as pltpu
from jax.sharding import PartitionSpec as P

L1_DEV = 4
PRIOR = 8.0
PLANE = 4
LANES = 128
MESH = pl.DeviceIdType.MESH


def split_counts(count, rows):
    high = count.astype(jnp.bfloat16).astype(jnp.float32)
    lane = lax.broadcasted_iota(jnp.int32, (rows, LANES), 1)
    return jnp.where(lane < LANES // 2, high, count - high)


def joined_counts(tail):
    return tail[:, :1] + tail[:, LANES // 2:LANES // 2 + 1]


def kernel(planes, rows_chunk, cols_chunk,
           emb_hbm, level_ref, cen_ref, empty_ref, reseed_ref,
           out_ref, count_ref,
           emb, cent, weights, lane_counts, parts, from_twin, to_mate, from_mate, to_plane, from_plane, own,
           emb_sem, z_send, z_recv, y_send, y_recv, t_send, t_recv, u_send, u_recv,
           rt_send, rt_recv, ry_send, ry_recv, rz_send, rz_recv):
    group = lax.axis_index("groups")
    me = lax.axis_index("owners")
    plane, lane = me // PLANE, me % PLANE
    y, c = lane // 2, lane % 2
    twin = plane * PLANE + y * 2 + (1 - c)
    mate = plane * PLANE + (1 - y) * 2 + c
    local, width = cen_ref.shape
    row_count = emb.shape[0]
    sub = local // L1_DEV
    block = PLANE * local
    wide = width + LANES

    def plane_mate(steps):
        return ((plane + steps) % planes) * PLANE + lane

    load = pltpu.make_async_copy(emb_hbm, emb, emb_sem)
    load.start()

    barrier = pltpu.get_barrier_semaphore()

    def greet(other):
        pl.semaphore_signal(barrier, inc=1, device_id=(group, other), device_id_type=MESH)

    greet(twin)
    greet(mate)
    for step in range(1, planes):
        greet(plane_mate(step))
    cent[0, c, y] = cen_ref[...].astype(jnp.bfloat16)
    pl.semaphore_wait(barrier, planes + 1)

    def remote(src, dst, send, recv, other):
        return pltpu.make_async_remote_copy(
            src_ref=src, dst_ref=dst, send_sem=send, recv_sem=recv,
            device_id=(group, other), device_id_type=MESH)

    def z_copy(s):
        return remote(cent.at[0, c, y], cent.at[s, c, y], z_send.at[s], z_recv.at[s], plane_mate(planes - s))

    def y_copy(s):
        return remote(cent.at[s, c, y], cent.at[s, c, y], y_send.at[s], y_recv.at[s], mate)

    def t_copy(s):
        return remote(cent.at[s, c, y], cent.at[s, c, y], t_send.at[s], t_recv.at[s], twin)

    def u_copy(s):
        return remote(cent.at[s, c, 1 - y], cent.at[s, c, 1 - y], u_send.at[s], u_recv.at[s], twin)

    def rt_copy(s):
        return remote(parts.at[s, 1 - c], from_twin.at[s], rt_send.at[s], rt_recv.at[s], twin)

    def ry_copy(s):
        return remote(to_mate.at[s], from_mate.at[s], ry_send.at[s], ry_recv.at[s], mate)

    def rz_copy(s):
        return remote(to_plane.at[s], from_plane.at[s], rz_send.at[s], rz_recv.at[s], plane_mate(s))

    y_copy(0).start()
    t_copy(0).start()
    for step in range(1, planes):
        z_copy(step).start()

    def spread_first(s):
        z_copy(s).wait_recv()
        y_copy(s).start()
        t_copy(s).start()

    def spread_second(s):
        y_copy(s).wait_recv()
        u_copy(s).start()

    def arrived(s):
        t_copy(s).wait_recv()
        u_copy(s).wait_recv()

    def replaced(first, rows, ids):
        hit = ids == empty_ref[...]
        row = jnp.sum(jnp.where(hit, reseed_ref[...] - me * row_count, 0), axis=1, keepdims=True)
        return jnp.sum(jnp.where(hit, 1, 0), axis=1, keepdims=True) > 0, row

    def weigh(s):
        target = (plane + s) % planes
        centroid = cent[s].reshape(block, width)
        as_f32 = centroid.astype(jnp.float32)
        half_norm = 0.5 * jnp.sum(as_f32 * as_f32, axis=1, keepdims=True)
        place = lax.broadcasted_iota(jnp.int32, (block, 1), 0)
        of_c, of_y, of_l = place // (2 * local), (place // local) % 2, place % local
        ids = target * block + (of_y * 2 + of_c) * local + of_l
        reseeded, source_row = replaced(0, block, ids)
        lane_counts[...] = jnp.zeros_like(lane_counts)

        @pl.loop(0, row_count // rows_chunk)
        def _(i):
            at = pl.ds(pl.multiple_of(i * rows_chunk, rows_chunk), rows_chunk)
            scores = lax.dot_general(
                cent[s].reshape(block, width), emb[at, :], (((1,), (1,)), ((), ())),
                preferred_element_type=jnp.float32)
            logits = (scores - half_norm) * (1.0 / math.sqrt(width))
            cluster = level_ref[:, at] - target * (PLANE * L1_DEV)
            picked = jnp.zeros((sub, rows_chunk), jnp.float32)
            order = []
            for g in range(PLANE * L1_DEV):
                gc, gy, gk = g // (2 * L1_DEV), (g // L1_DEV) % 2, g % L1_DEV
                order.append((gy * 2 + gc) * L1_DEV + gk)
            masks = [cluster == value for value in order]
            for g, mask in enumerate(masks):
                picked = jnp.where(mask, logits[g * sub:(g + 1) * sub], picked)
            raised = jnp.exp(picked - jnp.max(picked, axis=0, keepdims=True))
            soft = raised / jnp.sum(raised, axis=0, keepdims=True)
            spread = jnp.concatenate([jnp.where(mask, soft, 0.0) for mask in masks], axis=0)
            tally = lane_counts[...]
            for k in range(rows_chunk // LANES):
                tally = tally + spread[:, k * LANES:(k + 1) * LANES]
            lane_counts[...] = tally
            row = lax.broadcasted_iota(jnp.int32, (1, rows_chunk), 1) + i * rows_chunk
            chosen = jnp.where(row == source_row, 1.0, 0.0)
            weights[:, at] = jnp.where(reseeded, chosen, spread).astype(jnp.bfloat16)

    def collect(s):
        count = jnp.sum(lane_counts[...], axis=1, keepdims=True)
        parts[s, :, :, :, width:] = split_counts(count, block).astype(jnp.bfloat16).reshape(2, 2, local, LANES)

        @pl.loop(0, width // cols_chunk)
        def _(i):
            at = pl.ds(pl.multiple_of(i * cols_chunk, cols_chunk), cols_chunk)
            total = jnp.dot(weights[...], emb[:, at], preferred_element_type=jnp.float32)
            parts[s, :, :, :, at] = total.astype(jnp.bfloat16).reshape(2, 2, local, cols_chunk)

    def put(ref, s, value):
        tail = value[:, width:]
        ref[s, :, :width] = value[:, :width].astype(jnp.bfloat16)
        ref[s, :, width:] = split_counts(joined_counts(tail), local).astype(jnp.bfloat16)

    def reduce_second(s):
        rt_copy(s).wait_recv()
        value = parts[s, c, 1 - y].astype(jnp.float32) + from_twin[s, 1 - y].astype(jnp.float32)
        put(to_mate, s, value)
        ry_copy(s).start()

    def reduce_third(s):
        ry_copy(s).wait_recv()
        value = (parts[s, c, y].astype(jnp.float32) + from_twin[s, y].astype(jnp.float32)
                 + from_mate[s].astype(jnp.float32))

        @pl.when(s == 0)
        def _():
            own[...] = value

        @pl.when(s > 0)
        def _():
            put(to_plane, s, value)
            rz_copy(s).start()

    spread_second(0)
    spread_first(1)
    load.wait()

    @pl.loop(0, planes)
    def _(s):
        arrived(s)
        weigh(s)

        @pl.when(s >= 1)
        def _():
            reduce_second(s - 1)

        @pl.when(s + 1 < planes)
        def _():
            spread_second(s + 1)

        @pl.when(s + 2 < planes)
        def _():
            spread_first(s + 2)

        collect(s)
        rt_copy(s).start()

        @pl.when(s >= 1)
        def _():
            reduce_third(s - 1)

    reduce_second(planes - 1)
    reduce_third(planes - 1)

    total = own[...]
    for step in range(1, planes):
        rz_copy(step).wait_recv()
        total = total + from_plane[step].astype(jnp.float32)
    count = joined_counts(total[:, width:])
    ids = me * local + lax.broadcasted_iota(jnp.int32, (local, 1), 0)
    reseeded, _ = replaced(0, local, ids)
    sums = total[:, :width]
    updated = (sums + PRIOR * cen_ref[...]) / (count + PRIOR)
    out_ref[...] = jnp.where(reseeded, sums, updated)
    diagonal = (lax.broadcasted_iota(jnp.int32, (local, local), 0)
                == lax.broadcasted_iota(jnp.int32, (local, local), 1))
    count_ref[...] = jnp.sum(jnp.where(diagonal, count, 0.0), axis=0, keepdims=True)

    @pl.loop(0, planes)
    def _(s):
        y_copy(s).wait_send()
        t_copy(s).wait_send()
        u_copy(s).wait_send()
        rt_copy(s).wait_send()
        ry_copy(s).wait_send()

        @pl.when(s > 0)
        def _():
            z_copy(s).wait_send()
            rz_copy(s).wait_send()


def shards(owners, embeddings, level_ids, centroids, empty_ids, reseed_rows):
    row_count, width = embeddings.shape
    local = centroids.shape[0]
    planes = owners // PLANE
    wide = width + LANES
    block = PLANE * local
    bf16, f32 = jnp.bfloat16, jnp.float32
    vmem = pl.BlockSpec(memory_space=pltpu.VMEM)
    sem = pltpu.SemaphoreType.DMA((planes,))
    new_centroids, counts = pl.pallas_call(
        functools.partial(kernel, planes, 512, 512),
        out_shape=(jax.ShapeDtypeStruct((local, width), f32), jax.ShapeDtypeStruct((1, local), f32)),
        in_specs=[pl.BlockSpec(memory_space=pl.ANY), vmem, vmem, vmem, vmem],
        out_specs=(vmem, vmem),
        scratch_shapes=[
            pltpu.VMEM((row_count, width), bf16),
            pltpu.VMEM((planes, 2, 2, local, width), bf16),
            pltpu.VMEM((block, row_count), bf16),
            pltpu.VMEM((block, LANES), f32),
            pltpu.VMEM((planes, 2, 2, local, wide), bf16),
            pltpu.VMEM((planes, 2, local, wide), bf16),
            pltpu.VMEM((planes, local, wide), bf16),
            pltpu.VMEM((planes, local, wide), bf16),
            pltpu.VMEM((planes, local, wide), bf16),
            pltpu.VMEM((planes, local, wide), bf16),
            pltpu.VMEM((local, wide), f32),
            pltpu.SemaphoreType.DMA,
        ] + [sem] * 14,
        compiler_params=pltpu.CompilerParams(
            collective_id=0, has_side_effects=True, vmem_limit_bytes=48 * 1024 * 1024),
        cost_estimate=pl.CostEstimate(
            flops=4 * row_count * width * owners * local, transcendentals=row_count * 64,
            bytes_accessed=2 * row_count * width),
    )(embeddings, level_ids.reshape(1, -1), centroids, empty_ids.reshape(1, -1), reseed_rows.reshape(1, -1))
    return new_centroids, counts.reshape(-1)


def solution(mesh):
    in_specs = (
        P(("groups", "owners"), None),
        P(("groups", "owners")),
        P(("groups", "owners"), None),
        P("groups"),
        P("groups"),
    )
    out_specs = (P(("groups", "owners"), None), P(("groups", "owners")))
    return jax.shard_map(functools.partial(shards, mesh.shape["owners"]), mesh=mesh,
                         in_specs=in_specs, out_specs=out_specs, check_vma=False)
```

```python
import functools
import math

import jax
import jax.numpy as jnp
from jax import lax
from jax.experimental import pallas as pl
from jax.experimental.pallas import tpu as pltpu
from jax.sharding import PartitionSpec as P

L1_DEV = 4
PRIOR = 8.0
PLANE = 4
LANES = 128
MESH = pl.DeviceIdType.MESH


def split_counts(count, rows):
    high = count.astype(jnp.bfloat16).astype(jnp.float32)
    lane = lax.broadcasted_iota(jnp.int32, (rows, LANES), 1)
    return jnp.where(lane < LANES // 2, high, count - high)


def joined_counts(tail):
    return tail[:, :1] + tail[:, LANES // 2:LANES // 2 + 1]


def kernel(planes, rows_chunk, cols_chunk,
           emb_hbm, level_hbm, cen_hbm, empty_hbm, reseed_hbm,
           out_ref, count_ref,
           emb, level_ref, cen_ref, empty_ref, reseed_ref,
           cent, weights, lane_counts, parts, from_twin, to_mate, from_mate, to_plane, from_plane, own,
           load_sem, z_send, z_recv, y_send, y_recv, t_send, t_recv, u_send, u_recv,
           rt_send, rt_recv, ry_send, ry_recv, rz_send, rz_recv):
    group = lax.axis_index("groups")
    me = lax.axis_index("owners")
    plane, lane = me // PLANE, me % PLANE
    y, c = lane // 2, lane % 2
    twin = plane * PLANE + y * 2 + (1 - c)
    mate = plane * PLANE + (1 - y) * 2 + c
    local, width = cen_ref.shape
    row_count = emb.shape[0]
    sub = local // L1_DEV
    block = PLANE * local

    def plane_mate(p):
        return p * PLANE + lane

    loads = [pltpu.make_async_copy(src, dst, load_sem.at[i]) for i, (src, dst) in enumerate([
        (cen_hbm, cen_ref), (level_hbm, level_ref), (empty_hbm, empty_ref), (reseed_hbm, reseed_ref),
        (emb_hbm, emb)])]
    for load in loads:
        load.start()

    barrier = pltpu.get_barrier_semaphore()

    def greet(other):
        pl.semaphore_signal(barrier, inc=1, device_id=(group, other), device_id_type=MESH)

    greet(twin)
    greet(mate)
    for step in range(1, planes):
        greet(plane_mate((plane + step) % planes))
    loads[0].wait()
    cent[plane, c, y] = cen_ref[...].astype(jnp.bfloat16)
    pl.semaphore_wait(barrier, planes + 1)

    both = jnp.minimum(plane, planes - 1 - plane)

    def nth(i):
        near = jnp.where(i % 2 == 1, plane + (i + 1) // 2, plane - i // 2)
        far = jnp.where(plane < planes - 1 - plane, plane + i - both, plane - i + both)
        return jnp.where(i <= 2 * both, near, far)

    def remote(src, dst, send, recv, other):
        return pltpu.make_async_remote_copy(
            src_ref=src, dst_ref=dst, send_sem=send, recv_sem=recv,
            device_id=(group, other), device_id_type=MESH)

    def up_copy(p):
        return remote(cent.at[p, c, y], cent.at[p, c, y], z_send.at[p, 0], z_recv.at[p], plane_mate(plane + 1))

    def down_copy(p):
        return remote(cent.at[p, c, y], cent.at[p, c, y], z_send.at[p, 1], z_recv.at[p], plane_mate(plane - 1))

    def y_copy(p):
        return remote(cent.at[p, c, y], cent.at[p, c, y], y_send.at[p], y_recv.at[p], mate)

    def t_copy(p):
        return remote(cent.at[p, c, y], cent.at[p, c, y], t_send.at[p], t_recv.at[p], twin)

    def u_copy(p):
        return remote(cent.at[p, c, 1 - y], cent.at[p, c, 1 - y], u_send.at[p], u_recv.at[p], twin)

    def rt_copy(p):
        return remote(parts.at[p, 1 - c], from_twin.at[p], rt_send.at[p], rt_recv.at[p], twin)

    def ry_copy(p):
        return remote(to_mate.at[p], from_mate.at[p], ry_send.at[p], ry_recv.at[p], mate)

    def rz_copy(p):
        return remote(to_plane.at[p], from_plane.at[plane], rz_send.at[p], rz_recv.at[plane], plane_mate(p))

    def rz_arrival(p):
        return remote(to_plane.at[p], from_plane.at[p], rz_send.at[p], rz_recv.at[p], plane_mate(p))

    def relay(p):
        @pl.when((p <= plane) & (plane < planes - 1))
        def _():
            up_copy(p).start()

        @pl.when((p >= plane) & (plane > 0))
        def _():
            down_copy(p).start()

    def relay_sent(p):
        @pl.when((p <= plane) & (plane < planes - 1))
        def _():
            up_copy(p).wait_send()

        @pl.when((p >= plane) & (plane > 0))
        def _():
            down_copy(p).wait_send()

    y_copy(plane).start()
    relay(plane)
    t_copy(plane).start()

    def spread_first(p):
        up_copy(p).wait_recv()
        relay(p)
        y_copy(p).start()
        t_copy(p).start()

    def spread_second(p):
        y_copy(p).wait_recv()
        u_copy(p).start()

    def arrived(p):
        t_copy(p).wait_recv()
        u_copy(p).wait_recv()

    def replaced(ids):
        hit = ids == empty_ref[...]
        row = jnp.sum(jnp.where(hit, reseed_ref[...] - me * row_count, 0), axis=1, keepdims=True)
        return jnp.sum(jnp.where(hit, 1, 0), axis=1, keepdims=True) > 0, row

    def weigh(s):
        target = s
        centroid = cent[s].reshape(block, width)
        as_f32 = centroid.astype(jnp.float32)
        half_norm = 0.5 * jnp.sum(as_f32 * as_f32, axis=1, keepdims=True)
        place = lax.broadcasted_iota(jnp.int32, (block, 1), 0)
        of_c, of_y, of_l = place // (2 * local), (place // local) % 2, place % local
        ids = target * block + (of_y * 2 + of_c) * local + of_l
        reseeded, source_row = replaced(ids)
        lane_counts[...] = jnp.zeros_like(lane_counts)

        @pl.loop(0, row_count // rows_chunk)
        def _(i):
            at = pl.ds(pl.multiple_of(i * rows_chunk, rows_chunk), rows_chunk)
            scores = lax.dot_general(
                cent[s].reshape(block, width), emb[at, :], (((1,), (1,)), ((), ())),
                preferred_element_type=jnp.float32)
            logits = (scores - half_norm) * (1.0 / math.sqrt(width))
            cluster = level_ref[:, at] - target * (PLANE * L1_DEV)
            picked = jnp.zeros((sub, rows_chunk), jnp.float32)
            order = []
            for g in range(PLANE * L1_DEV):
                gc, gy, gk = g // (2 * L1_DEV), (g // L1_DEV) % 2, g % L1_DEV
                order.append((gy * 2 + gc) * L1_DEV + gk)
            masks = [cluster == value for value in order]
            for g, mask in enumerate(masks):
                picked = jnp.where(mask, logits[g * sub:(g + 1) * sub], picked)
            raised = jnp.exp(picked - jnp.max(picked, axis=0, keepdims=True))
            soft = raised / jnp.sum(raised, axis=0, keepdims=True)
            spread = jnp.concatenate([jnp.where(mask, soft, 0.0) for mask in masks], axis=0)
            tally = lane_counts[...]
            for k in range(rows_chunk // LANES):
                tally = tally + spread[:, k * LANES:(k + 1) * LANES]
            lane_counts[...] = tally
            row = lax.broadcasted_iota(jnp.int32, (1, rows_chunk), 1) + i * rows_chunk
            chosen = jnp.where(row == source_row, 1.0, 0.0)
            weights[:, at] = jnp.where(reseeded, chosen, spread).astype(jnp.bfloat16)

    def collect(s):
        count = jnp.sum(lane_counts[...], axis=1, keepdims=True)
        parts[s, :, :, :, width:] = split_counts(count, block).astype(jnp.bfloat16).reshape(2, 2, local, LANES)

        @pl.loop(0, width // cols_chunk)
        def _(i):
            at = pl.ds(pl.multiple_of(i * cols_chunk, cols_chunk), cols_chunk)
            total = jnp.dot(weights[...], emb[:, at], preferred_element_type=jnp.float32)
            parts[s, :, :, :, at] = total.astype(jnp.bfloat16).reshape(2, 2, local, cols_chunk)

    def put(ref, s, value):
        tail = value[:, width:]
        ref[s, :, :width] = value[:, :width].astype(jnp.bfloat16)
        ref[s, :, width:] = split_counts(joined_counts(tail), local).astype(jnp.bfloat16)

    def reduce_second(s):
        rt_copy(s).wait_recv()
        value = parts[s, c, 1 - y].astype(jnp.float32) + from_twin[s, 1 - y].astype(jnp.float32)
        put(to_mate, s, value)
        ry_copy(s).start()

    def reduce_third(s):
        ry_copy(s).wait_recv()
        value = (parts[s, c, y].astype(jnp.float32) + from_twin[s, y].astype(jnp.float32)
                 + from_mate[s].astype(jnp.float32))

        @pl.when(s == plane)
        def _():
            own[...] = value

        @pl.when(s != plane)
        def _():
            put(to_plane, s, value)
            rz_copy(s).start()

    last = planes - 1

    def turn(k):
        return nth(jnp.where(k == last, 0, k + 1))

    spread_first(nth(1))
    spread_second(plane)
    spread_first(nth(2))
    spread_second(nth(1))
    for load in loads[1:]:
        load.wait()

    @pl.loop(0, planes)
    def _(k):
        p = turn(k)
        arrived(p)
        weigh(p)

        @pl.when(k >= 2)
        def _():
            reduce_third(turn(k - 2))

        @pl.when(k >= 1)
        def _():
            reduce_second(turn(k - 1))

        @pl.when(k + 3 <= last)
        def _():
            spread_first(nth(k + 3))

        @pl.when(k + 2 <= last)
        def _():
            spread_second(nth(k + 2))

        collect(p)
        rt_copy(p).start()

    reduce_second(plane)
    reduce_third(turn(last - 1))
    reduce_third(plane)

    total = own[...]
    for step in range(1, planes):
        p = nth(step)
        rz_arrival(p).wait_recv()
        total = total + from_plane[p].astype(jnp.float32)
    count = joined_counts(total[:, width:])
    ids = me * local + lax.broadcasted_iota(jnp.int32, (local, 1), 0)
    reseeded, _ = replaced(ids)
    sums = total[:, :width]
    updated = (sums + PRIOR * cen_ref[...]) / (count + PRIOR)
    out_ref[...] = jnp.where(reseeded, sums, updated)
    diagonal = (lax.broadcasted_iota(jnp.int32, (local, local), 0)
                == lax.broadcasted_iota(jnp.int32, (local, local), 1))
    count_ref[...] = jnp.sum(jnp.where(diagonal, count, 0.0), axis=0, keepdims=True)

    @pl.loop(0, planes)
    def _(p):
        y_copy(p).wait_send()
        t_copy(p).wait_send()
        u_copy(p).wait_send()
        relay_sent(p)
        rt_copy(p).wait_send()
        ry_copy(p).wait_send()

        @pl.when(p != plane)
        def _():
            rz_copy(p).wait_send()


def shards(owners, embeddings, level_ids, centroids, empty_ids, reseed_rows):
    row_count, width = embeddings.shape
    local = centroids.shape[0]
    planes = owners // PLANE
    wide = width + LANES
    block = PLANE * local
    bf16, f32 = jnp.bfloat16, jnp.float32
    vmem = pl.BlockSpec(memory_space=pltpu.VMEM)
    sem = pltpu.SemaphoreType.DMA((planes,))
    new_centroids, counts = pl.pallas_call(
        functools.partial(kernel, planes, 512, 512),
        out_shape=(jax.ShapeDtypeStruct((local, width), f32), jax.ShapeDtypeStruct((1, local), f32)),
        in_specs=[pl.BlockSpec(memory_space=pl.ANY)] * 5,
        out_specs=(vmem, vmem),
        scratch_shapes=[
            pltpu.VMEM((row_count, width), bf16),
            pltpu.VMEM((1, row_count), jnp.int32),
            pltpu.VMEM((local, width), f32),
            pltpu.VMEM((1, empty_ids.shape[0]), jnp.int32),
            pltpu.VMEM((1, empty_ids.shape[0]), jnp.int32),
            pltpu.VMEM((planes, 2, 2, local, width), bf16),
            pltpu.VMEM((block, row_count), bf16),
            pltpu.VMEM((block, LANES), f32),
            pltpu.VMEM((planes, 2, 2, local, wide), bf16),
            pltpu.VMEM((planes, 2, local, wide), bf16),
            pltpu.VMEM((planes, local, wide), bf16),
            pltpu.VMEM((planes, local, wide), bf16),
            pltpu.VMEM((planes, local, wide), bf16),
            pltpu.VMEM((planes, local, wide), bf16),
            pltpu.VMEM((local, wide), f32),
            pltpu.SemaphoreType.DMA((5,)),
            pltpu.SemaphoreType.DMA((planes, 2)),
        ] + [sem] * 13,
        compiler_params=pltpu.CompilerParams(
            collective_id=0, has_side_effects=True, vmem_limit_bytes=60 * 1024 * 1024),
        cost_estimate=pl.CostEstimate(
            flops=4 * row_count * width * owners * local, transcendentals=row_count * 64,
            bytes_accessed=2 * row_count * width),
    )(embeddings, level_ids.reshape(1, -1), centroids, empty_ids.reshape(1, -1), reseed_rows.reshape(1, -1))
    return new_centroids, counts.reshape(-1)


def solution(mesh):
    in_specs = (
        P(("groups", "owners"), None),
        P(("groups", "owners")),
        P(("groups", "owners"), None),
        P("groups"),
        P("groups"),
    )
    out_specs = (P(("groups", "owners"), None), P(("groups", "owners")))
    return jax.shard_map(functools.partial(shards, mesh.shape["owners"]), mesh=mesh,
                         in_specs=in_specs, out_specs=out_specs, check_vma=False)
```

```python
import functools
import math

import jax
import jax.numpy as jnp
from jax import lax
from jax.experimental import pallas as pl
from jax.experimental.pallas import tpu as pltpu
from jax.sharding import PartitionSpec as P

L1_DEV = 4
PRIOR = 8.0
PLANE = 4
LANES = 128
MESH = pl.DeviceIdType.MESH


def split_counts(count, rows):
    high = count.astype(jnp.bfloat16).astype(jnp.float32)
    lane = lax.broadcasted_iota(jnp.int32, (rows, LANES), 1)
    return jnp.where(lane < LANES // 2, high, count - high)


def joined_counts(tail):
    return tail[:, :1] + tail[:, LANES // 2:LANES // 2 + 1]


def kernel(planes, rows_chunk, cols_chunk,
           emb_hbm, level_hbm, cen_hbm, empty_hbm, reseed_hbm,
           out_ref, count_ref,
           emb, level_ref, cen_ref, empty_ref, reseed_ref,
           cent, weights, lane_counts, parts, from_twin, to_mate, from_mate, to_plane, from_plane, own,
           load_sem, z_send, z_recv, y_send, y_recv, t_send, t_recv, u_send, u_recv,
           rt_send, rt_recv, ry_send, ry_recv, rz_send, rz_recv):
    group = lax.axis_index("groups")
    me = lax.axis_index("owners")
    plane, lane = me // PLANE, me % PLANE
    y, c = lane // 2, lane % 2
    twin = plane * PLANE + y * 2 + (1 - c)
    mate = plane * PLANE + (1 - y) * 2 + c
    local, width = cen_ref.shape
    row_count = emb.shape[0]
    sub = local // L1_DEV
    block = PLANE * local

    def plane_mate(p):
        return p * PLANE + lane

    loads = [pltpu.make_async_copy(src, dst, load_sem.at[i]) for i, (src, dst) in enumerate([
        (cen_hbm, cen_ref), (level_hbm, level_ref), (empty_hbm, empty_ref), (reseed_hbm, reseed_ref),
        (emb_hbm, emb)])]
    for load in loads:
        load.start()

    barrier = pltpu.get_barrier_semaphore()

    def greet(other):
        pl.semaphore_signal(barrier, inc=1, device_id=(group, other), device_id_type=MESH)

    greet(twin)
    greet(mate)
    for step in range(1, planes):
        greet(plane_mate((plane + step) % planes))
    loads[0].wait()
    cent[plane, c, y] = cen_ref[...].astype(jnp.bfloat16)
    pl.semaphore_wait(barrier, planes + 1)

    both = jnp.minimum(plane, planes - 1 - plane)

    def nth(i):
        near = jnp.where(i % 2 == 1, plane + (i + 1) // 2, plane - i // 2)
        far = jnp.where(plane < planes - 1 - plane, plane + i - both, plane - i + both)
        return jnp.where(i <= 2 * both, near, far)

    def remote(src, dst, send, recv, other):
        return pltpu.make_async_remote_copy(
            src_ref=src, dst_ref=dst, send_sem=send, recv_sem=recv,
            device_id=(group, other), device_id_type=MESH)

    def up_copy(p):
        return remote(cent.at[p, c, y], cent.at[p, c, y], z_send.at[p, 0], z_recv.at[p], plane_mate(plane + 1))

    def down_copy(p):
        return remote(cent.at[p, c, y], cent.at[p, c, y], z_send.at[p, 1], z_recv.at[p], plane_mate(plane - 1))

    def y_copy(p):
        return remote(cent.at[p, c, y], cent.at[p, c, y], y_send.at[p], y_recv.at[p], mate)

    def t_copy(p):
        return remote(cent.at[p, c, y], cent.at[p, c, y], t_send.at[p], t_recv.at[p], twin)

    def u_copy(p):
        return remote(cent.at[p, c, 1 - y], cent.at[p, c, 1 - y], u_send.at[p], u_recv.at[p], twin)

    def rt_copy(p):
        return remote(parts.at[p, 1 - c], from_twin.at[p], rt_send.at[p], rt_recv.at[p], twin)

    def ry_copy(p):
        return remote(to_mate.at[p], from_mate.at[p], ry_send.at[p], ry_recv.at[p], mate)

    def rz_copy(p):
        return remote(to_plane.at[p], from_plane.at[plane], rz_send.at[p], rz_recv.at[plane], plane_mate(p))

    def rz_arrival(p):
        return remote(to_plane.at[p], from_plane.at[p], rz_send.at[p], rz_recv.at[p], plane_mate(p))

    def relay(p):
        @pl.when((p <= plane) & (plane < planes - 1))
        def _():
            up_copy(p).start()

        @pl.when((p >= plane) & (plane > 0))
        def _():
            down_copy(p).start()

    def relay_sent(p):
        @pl.when((p <= plane) & (plane < planes - 1))
        def _():
            up_copy(p).wait_send()

        @pl.when((p >= plane) & (plane > 0))
        def _():
            down_copy(p).wait_send()

    y_copy(plane).start()
    relay(plane)
    t_copy(plane).start()

    def spread_first(p):
        up_copy(p).wait_recv()
        relay(p)
        y_copy(p).start()
        t_copy(p).start()

    def spread_second(p):
        y_copy(p).wait_recv()
        u_copy(p).start()

    def arrived(p):
        t_copy(p).wait_recv()
        u_copy(p).wait_recv()

    def replaced(ids):
        hit = ids == empty_ref[...]
        row = jnp.sum(jnp.where(hit, reseed_ref[...] - me * row_count, 0), axis=1, keepdims=True)
        return jnp.sum(jnp.where(hit, 1, 0), axis=1, keepdims=True) > 0, row

    def weigh(s):
        target = s
        centroid = cent[s].reshape(block, width)
        as_f32 = centroid.astype(jnp.float32)
        half_norm = 0.5 * jnp.sum(as_f32 * as_f32, axis=1, keepdims=True)
        place = lax.broadcasted_iota(jnp.int32, (block, 1), 0)
        of_c, of_y, of_l = place // (2 * local), (place // local) % 2, place % local
        ids = target * block + (of_y * 2 + of_c) * local + of_l
        reseeded, source_row = replaced(ids)
        lane_counts[...] = jnp.zeros_like(lane_counts)

        @pl.loop(0, row_count // rows_chunk)
        def _(i):
            at = pl.ds(pl.multiple_of(i * rows_chunk, rows_chunk), rows_chunk)
            scores = lax.dot_general(
                cent[s].reshape(block, width), emb[at, :], (((1,), (1,)), ((), ())),
                preferred_element_type=jnp.float32)
            logits = (scores - half_norm) * (1.0 / math.sqrt(width))
            cluster = level_ref[:, at] - target * (PLANE * L1_DEV)
            picked = jnp.zeros((sub, rows_chunk), jnp.float32)
            order = []
            for g in range(PLANE * L1_DEV):
                gc, gy, gk = g // (2 * L1_DEV), (g // L1_DEV) % 2, g % L1_DEV
                order.append((gy * 2 + gc) * L1_DEV + gk)
            masks = [cluster == value for value in order]
            for g, mask in enumerate(masks):
                picked = jnp.where(mask, logits[g * sub:(g + 1) * sub], picked)
            raised = jnp.exp(picked - jnp.max(picked, axis=0, keepdims=True))
            soft = raised / jnp.sum(raised, axis=0, keepdims=True)
            spread = jnp.concatenate([jnp.where(mask, soft, 0.0) for mask in masks], axis=0)
            tally = lane_counts[...]
            for k in range(rows_chunk // LANES):
                tally = tally + spread[:, k * LANES:(k + 1) * LANES]
            lane_counts[...] = tally
            row = lax.broadcasted_iota(jnp.int32, (1, rows_chunk), 1) + i * rows_chunk
            chosen = jnp.where(row == source_row, 1.0, 0.0)
            weights[:, at] = jnp.where(reseeded, chosen, spread).astype(jnp.bfloat16)

    def collect(s):
        count = jnp.sum(lane_counts[...], axis=1, keepdims=True)
        parts[s, :, :, :, width:] = split_counts(count, block).astype(jnp.bfloat16).reshape(2, 2, local, LANES)

        @pl.loop(0, width // cols_chunk)
        def _(i):
            at = pl.ds(pl.multiple_of(i * cols_chunk, cols_chunk), cols_chunk)
            total = jnp.dot(weights[...], emb[:, at], preferred_element_type=jnp.float32)
            parts[s, :, :, :, at] = total.astype(jnp.bfloat16).reshape(2, 2, local, cols_chunk)

    def put(ref, s, value):
        tail = value[:, width:]
        ref[s, :, :width] = value[:, :width].astype(jnp.bfloat16)
        ref[s, :, width:] = split_counts(joined_counts(tail), local).astype(jnp.bfloat16)

    def reduce_second(s):
        rt_copy(s).wait_recv()
        value = parts[s, c, 1 - y].astype(jnp.float32) + from_twin[s, 1 - y].astype(jnp.float32)
        put(to_mate, s, value)
        ry_copy(s).start()

    def reduce_third(s):
        ry_copy(s).wait_recv()
        value = (parts[s, c, y].astype(jnp.float32) + from_twin[s, y].astype(jnp.float32)
                 + from_mate[s].astype(jnp.float32))

        @pl.when(s == plane)
        def _():
            own[...] = value

        @pl.when(s != plane)
        def _():
            put(to_plane, s, value)
            rz_copy(s).start()

    last = planes - 1

    def turn(k):
        return nth(jnp.where(k == 0, 0, jnp.where(k == last, 1, k + 1)))

    spread_second(plane)
    spread_first(nth(1))
    for load in loads[1:]:
        load.wait()

    @pl.loop(0, planes)
    def _(k):
        p = turn(k)
        arrived(p)
        weigh(p)

        @pl.when(k >= 2)
        def _():
            reduce_third(turn(k - 2))

        @pl.when(k >= 1)
        def _():
            reduce_second(turn(k - 1))

        @pl.when(k == 0)
        def _():
            spread_second(nth(1))
            spread_first(nth(2))

        @pl.when((k >= 1) & (k + 2 <= last))
        def _():
            spread_second(nth(k + 2))

        @pl.when((k >= 1) & (k + 3 <= last))
        def _():
            spread_first(nth(k + 3))

        collect(p)
        rt_copy(p).start()

        @pl.when(k == 0)
        def _():
            spread_second(nth(2))
            spread_first(nth(3))


    reduce_second(turn(last))
    reduce_third(turn(last - 1))
    reduce_third(turn(last))

    total = own[...]
    for step in range(1, planes):
        p = nth(step)
        rz_arrival(p).wait_recv()
        total = total + from_plane[p].astype(jnp.float32)
    count = joined_counts(total[:, width:])
    ids = me * local + lax.broadcasted_iota(jnp.int32, (local, 1), 0)
    reseeded, _ = replaced(ids)
    sums = total[:, :width]
    updated = (sums + PRIOR * cen_ref[...]) / (count + PRIOR)
    out_ref[...] = jnp.where(reseeded, sums, updated)
    diagonal = (lax.broadcasted_iota(jnp.int32, (local, local), 0)
                == lax.broadcasted_iota(jnp.int32, (local, local), 1))
    count_ref[...] = jnp.sum(jnp.where(diagonal, count, 0.0), axis=0, keepdims=True)

    @pl.loop(0, planes)
    def _(p):
        y_copy(p).wait_send()
        t_copy(p).wait_send()
        u_copy(p).wait_send()
        relay_sent(p)
        rt_copy(p).wait_send()
        ry_copy(p).wait_send()

        @pl.when(p != plane)
        def _():
            rz_copy(p).wait_send()


def shards(owners, embeddings, level_ids, centroids, empty_ids, reseed_rows):
    row_count, width = embeddings.shape
    local = centroids.shape[0]
    planes = owners // PLANE
    wide = width + LANES
    block = PLANE * local
    bf16, f32 = jnp.bfloat16, jnp.float32
    vmem = pl.BlockSpec(memory_space=pltpu.VMEM)
    sem = pltpu.SemaphoreType.DMA((planes,))
    new_centroids, counts = pl.pallas_call(
        functools.partial(kernel, planes, row_count, width),
        out_shape=(jax.ShapeDtypeStruct((local, width), f32), jax.ShapeDtypeStruct((1, local), f32)),
        in_specs=[pl.BlockSpec(memory_space=pl.ANY)] * 5,
        out_specs=(vmem, vmem),
        scratch_shapes=[
            pltpu.VMEM((row_count, width), bf16),
            pltpu.VMEM((1, row_count), jnp.int32),
            pltpu.VMEM((local, width), f32),
            pltpu.VMEM((1, empty_ids.shape[0]), jnp.int32),
            pltpu.VMEM((1, empty_ids.shape[0]), jnp.int32),
            pltpu.VMEM((planes, 2, 2, local, width), bf16),
            pltpu.VMEM((block, row_count), bf16),
            pltpu.VMEM((block, LANES), f32),
            pltpu.VMEM((planes, 2, 2, local, wide), bf16),
            pltpu.VMEM((planes, 2, local, wide), bf16),
            pltpu.VMEM((planes, local, wide), bf16),
            pltpu.VMEM((planes, local, wide), bf16),
            pltpu.VMEM((planes, local, wide), bf16),
            pltpu.VMEM((planes, local, wide), bf16),
            pltpu.VMEM((local, wide), f32),
            pltpu.SemaphoreType.DMA((5,)),
            pltpu.SemaphoreType.DMA((planes, 2)),
        ] + [sem] * 13,
        compiler_params=pltpu.CompilerParams(
            collective_id=0, has_side_effects=True, vmem_limit_bytes=60 * 1024 * 1024),
        cost_estimate=pl.CostEstimate(
            flops=4 * row_count * width * owners * local, transcendentals=row_count * 64,
            bytes_accessed=2 * row_count * width),
    )(embeddings, level_ids.reshape(1, -1), centroids, empty_ids.reshape(1, -1), reseed_rows.reshape(1, -1))
    return new_centroids, counts.reshape(-1)


def solution(mesh):
    in_specs = (
        P(("groups", "owners"), None),
        P(("groups", "owners")),
        P(("groups", "owners"), None),
        P("groups"),
        P("groups"),
    )
    out_specs = (P(("groups", "owners"), None), P(("groups", "owners")))
    return jax.shard_map(functools.partial(shards, mesh.shape["owners"]), mesh=mesh,
                         in_specs=in_specs, out_specs=out_specs, check_vma=False)
```

```python
import functools
import math

import jax
import jax.numpy as jnp
from jax import lax
from jax.experimental import pallas as pl
from jax.experimental.pallas import tpu as pltpu
from jax.sharding import PartitionSpec as P

L1_DEV = 4
PRIOR = 8.0
PLANE = 4
LANES = 128
MESH = pl.DeviceIdType.MESH


def split_counts(count, rows):
    high = count.astype(jnp.bfloat16).astype(jnp.float32)
    lane = lax.broadcasted_iota(jnp.int32, (rows, LANES), 1)
    return jnp.where(lane < LANES // 2, high, count - high)


def joined_counts(tail):
    return tail[:, :1] + tail[:, LANES // 2:LANES // 2 + 1]


def kernel(planes, rows_chunk, cols_chunk,
           emb_hbm, level_hbm, cen_hbm, empty_hbm, reseed_hbm,
           out_ref, count_ref,
           emb, level_ref, cen_ref, empty_ref, reseed_ref,
           cent, weights, lane_counts, parts, from_twin, to_mate, from_mate, to_plane, from_plane, own,
           load_sem, z_send, z_recv, y_send, y_recv, t_send, t_recv, u_send, u_recv,
           rt_send, rt_recv, ry_send, ry_recv, rz_send, rz_recv):
    group = lax.axis_index("groups")
    me = lax.axis_index("owners")
    plane, lane = me // PLANE, me % PLANE
    y, c = lane // 2, lane % 2
    twin = plane * PLANE + y * 2 + (1 - c)
    mate = plane * PLANE + (1 - y) * 2 + c
    local, width = cen_ref.shape
    row_count = emb.shape[0]
    sub = local // L1_DEV
    block = PLANE * local

    def plane_mate(p):
        return p * PLANE + lane

    loads = [pltpu.make_async_copy(src, dst, load_sem.at[i]) for i, (src, dst) in enumerate([
        (cen_hbm, cen_ref), (level_hbm, level_ref), (empty_hbm, empty_ref), (reseed_hbm, reseed_ref),
        (emb_hbm, emb)])]
    for load in loads:
        load.start()

    barrier = pltpu.get_barrier_semaphore()

    def greet(other):
        pl.semaphore_signal(barrier, inc=1, device_id=(group, other), device_id_type=MESH)

    greet(twin)
    greet(mate)
    for step in range(1, planes):
        greet(plane_mate((plane + step) % planes))
    loads[0].wait()
    cent[plane, c, y] = cen_ref[...].astype(jnp.bfloat16)
    pl.semaphore_wait(barrier, planes + 1)

    both = jnp.minimum(plane, planes - 1 - plane)

    def nth(i):
        near = jnp.where(i % 2 == 1, plane + (i + 1) // 2, plane - i // 2)
        far = jnp.where(plane < planes - 1 - plane, plane + i - both, plane - i + both)
        return jnp.where(i <= 2 * both, near, far)

    def remote(src, dst, send, recv, other):
        return pltpu.make_async_remote_copy(
            src_ref=src, dst_ref=dst, send_sem=send, recv_sem=recv,
            device_id=(group, other), device_id_type=MESH)

    def up_copy(p):
        return remote(cent.at[p, c, y], cent.at[p, c, y], z_send.at[p, 0], z_recv.at[p], plane_mate(plane + 1))

    def down_copy(p):
        return remote(cent.at[p, c, y], cent.at[p, c, y], z_send.at[p, 1], z_recv.at[p], plane_mate(plane - 1))

    def y_copy(p):
        return remote(cent.at[p, c, y], cent.at[p, c, y], y_send.at[p], y_recv.at[p], mate)

    def t_copy(p):
        return remote(cent.at[p, c, y], cent.at[p, c, y], t_send.at[p], t_recv.at[p], twin)

    def u_copy(p):
        return remote(cent.at[p, c, 1 - y], cent.at[p, c, 1 - y], u_send.at[p], u_recv.at[p], twin)

    def rt_copy(p):
        return remote(parts.at[p, 1 - c], from_twin.at[p], rt_send.at[p], rt_recv.at[p], twin)

    def ry_copy(p):
        return remote(to_mate.at[p], from_mate.at[p], ry_send.at[p], ry_recv.at[p], mate)

    def rz_copy(p):
        return remote(to_plane.at[p], from_plane.at[plane], rz_send.at[p], rz_recv.at[plane], plane_mate(p))

    def rz_arrival(p):
        return remote(to_plane.at[p], from_plane.at[p], rz_send.at[p], rz_recv.at[p], plane_mate(p))

    def relay(p):
        @pl.when((p <= plane) & (plane < planes - 1))
        def _():
            up_copy(p).start()

        @pl.when((p >= plane) & (plane > 0))
        def _():
            down_copy(p).start()

    def relay_sent(p):
        @pl.when((p <= plane) & (plane < planes - 1))
        def _():
            up_copy(p).wait_send()

        @pl.when((p >= plane) & (plane > 0))
        def _():
            down_copy(p).wait_send()

    y_copy(plane).start()
    relay(plane)
    t_copy(plane).start()

    def spread_first(p):
        up_copy(p).wait_recv()
        relay(p)
        y_copy(p).start()
        t_copy(p).start()

    def spread_second(p):
        y_copy(p).wait_recv()
        u_copy(p).start()

    def arrived(p):
        t_copy(p).wait_recv()
        u_copy(p).wait_recv()

    def replaced(ids):
        hit = ids == empty_ref[...]
        row = jnp.sum(jnp.where(hit, reseed_ref[...] - me * row_count, 0), axis=1, keepdims=True)
        return jnp.sum(jnp.where(hit, 1, 0), axis=1, keepdims=True) > 0, row

    def weigh(s):
        target = s
        centroid = cent[s].reshape(block, width)
        as_f32 = centroid.astype(jnp.float32)
        half_norm = 0.5 * jnp.sum(as_f32 * as_f32, axis=1, keepdims=True)
        place = lax.broadcasted_iota(jnp.int32, (block, 1), 0)
        of_c, of_y, of_l = place // (2 * local), (place // local) % 2, place % local
        ids = target * block + (of_y * 2 + of_c) * local + of_l
        reseeded, source_row = replaced(ids)
        lane_counts[...] = jnp.zeros_like(lane_counts)

        @pl.loop(0, row_count // rows_chunk)
        def _(i):
            at = pl.ds(pl.multiple_of(i * rows_chunk, rows_chunk), rows_chunk)
            scores = lax.dot_general(
                cent[s].reshape(block, width), emb[at, :], (((1,), (1,)), ((), ())),
                preferred_element_type=jnp.float32)
            logits = (scores - half_norm) * (1.0 / math.sqrt(width))
            cluster = level_ref[:, at] - target * (PLANE * L1_DEV)
            picked = jnp.zeros((sub, rows_chunk), jnp.float32)
            order = []
            for g in range(PLANE * L1_DEV):
                gc, gy, gk = g // (2 * L1_DEV), (g // L1_DEV) % 2, g % L1_DEV
                order.append((gy * 2 + gc) * L1_DEV + gk)
            masks = [cluster == value for value in order]
            for g, mask in enumerate(masks):
                picked = jnp.where(mask, logits[g * sub:(g + 1) * sub], picked)
            raised = jnp.exp(picked - jnp.max(picked, axis=0, keepdims=True))
            soft = raised / jnp.sum(raised, axis=0, keepdims=True)
            spread = jnp.concatenate([jnp.where(mask, soft, 0.0) for mask in masks], axis=0)
            tally = lane_counts[...]
            for k in range(rows_chunk // LANES):
                tally = tally + spread[:, k * LANES:(k + 1) * LANES]
            lane_counts[...] = tally
            row = lax.broadcasted_iota(jnp.int32, (1, rows_chunk), 1) + i * rows_chunk
            chosen = jnp.where(row == source_row, 1.0, 0.0)
            weights[:, at] = jnp.where(reseeded, chosen, spread).astype(jnp.bfloat16)

    def collect(s):
        count = jnp.sum(lane_counts[...], axis=1, keepdims=True)
        parts[s, :, :, :, width:] = split_counts(count, block).astype(jnp.bfloat16).reshape(2, 2, local, LANES)

        @pl.loop(0, width // cols_chunk)
        def _(i):
            at = pl.ds(pl.multiple_of(i * cols_chunk, cols_chunk), cols_chunk)
            total = jnp.dot(weights[...], emb[:, at], preferred_element_type=jnp.float32)
            parts[s, :, :, :, at] = total.astype(jnp.bfloat16).reshape(2, 2, local, cols_chunk)

    def put(ref, s, value):
        tail = value[:, width:]
        ref[s, :, :width] = value[:, :width].astype(jnp.bfloat16)
        ref[s, :, width:] = split_counts(joined_counts(tail), local).astype(jnp.bfloat16)

    def reduce_second(s):
        rt_copy(s).wait_recv()
        value = parts[s, c, 1 - y].astype(jnp.float32) + from_twin[s, 1 - y].astype(jnp.float32)
        put(to_mate, s, value)
        ry_copy(s).start()

    def reduce_third(s):
        ry_copy(s).wait_recv()
        value = (parts[s, c, y].astype(jnp.float32) + from_twin[s, y].astype(jnp.float32)
                 + from_mate[s].astype(jnp.float32))

        @pl.when(s == plane)
        def _():
            own[...] = value

        @pl.when(s != plane)
        def _():
            put(to_plane, s, value)
            rz_copy(s).start()

    last = planes - 1

    def turn(k):
        return nth(jnp.where(k == 0, 0, jnp.where(k == last, 1, k + 1)))

    spread_second(plane)
    spread_first(nth(1))
    for load in loads[1:]:
        load.wait()

    @pl.loop(0, planes)
    def _(k):
        p = turn(k)
        arrived(p)
        weigh(p)

        @pl.when(k >= 1)
        def _():
            reduce_second(turn(k - 1))

        @pl.when(k == 0)
        def _():
            spread_second(nth(1))
            spread_first(nth(2))

        @pl.when((k >= 1) & (k + 2 <= last))
        def _():
            spread_second(nth(k + 2))

        @pl.when((k >= 1) & (k + 3 <= last))
        def _():
            spread_first(nth(k + 3))

        @pl.when(k >= 2)
        def _():
            reduce_third(turn(k - 2))

        collect(p)
        rt_copy(p).start()

        @pl.when(k == 0)
        def _():
            spread_second(nth(2))
            spread_first(nth(3))


    reduce_second(turn(last))
    reduce_third(turn(last - 1))
    reduce_third(turn(last))

    total = own[...]
    for step in range(1, planes):
        p = nth(step)
        rz_arrival(p).wait_recv()
        total = total + from_plane[p].astype(jnp.float32)
    count = joined_counts(total[:, width:])
    ids = me * local + lax.broadcasted_iota(jnp.int32, (local, 1), 0)
    reseeded, _ = replaced(ids)
    sums = total[:, :width]
    updated = (sums + PRIOR * cen_ref[...]) / (count + PRIOR)
    out_ref[...] = jnp.where(reseeded, sums, updated)
    diagonal = (lax.broadcasted_iota(jnp.int32, (local, local), 0)
                == lax.broadcasted_iota(jnp.int32, (local, local), 1))
    count_ref[...] = jnp.sum(jnp.where(diagonal, count, 0.0), axis=0, keepdims=True)

    @pl.loop(0, planes)
    def _(p):
        y_copy(p).wait_send()
        t_copy(p).wait_send()
        u_copy(p).wait_send()
        relay_sent(p)
        rt_copy(p).wait_send()
        ry_copy(p).wait_send()

        @pl.when(p != plane)
        def _():
            rz_copy(p).wait_send()


def shards(owners, embeddings, level_ids, centroids, empty_ids, reseed_rows):
    row_count, width = embeddings.shape
    local = centroids.shape[0]
    planes = owners // PLANE
    wide = width + LANES
    block = PLANE * local
    bf16, f32 = jnp.bfloat16, jnp.float32
    vmem = pl.BlockSpec(memory_space=pltpu.VMEM)
    sem = pltpu.SemaphoreType.DMA((planes,))
    new_centroids, counts = pl.pallas_call(
        functools.partial(kernel, planes, row_count, width),
        out_shape=(jax.ShapeDtypeStruct((local, width), f32), jax.ShapeDtypeStruct((1, local), f32)),
        in_specs=[pl.BlockSpec(memory_space=pl.ANY)] * 5,
        out_specs=(vmem, vmem),
        scratch_shapes=[
            pltpu.VMEM((row_count, width), bf16),
            pltpu.VMEM((1, row_count), jnp.int32),
            pltpu.VMEM((local, width), f32),
            pltpu.VMEM((1, empty_ids.shape[0]), jnp.int32),
            pltpu.VMEM((1, empty_ids.shape[0]), jnp.int32),
            pltpu.VMEM((planes, 2, 2, local, width), bf16),
            pltpu.VMEM((block, row_count), bf16),
            pltpu.VMEM((block, LANES), f32),
            pltpu.VMEM((planes, 2, 2, local, wide), bf16),
            pltpu.VMEM((planes, 2, local, wide), bf16),
            pltpu.VMEM((planes, local, wide), bf16),
            pltpu.VMEM((planes, local, wide), bf16),
            pltpu.VMEM((planes, local, wide), bf16),
            pltpu.VMEM((planes, local, wide), bf16),
            pltpu.VMEM((local, wide), f32),
            pltpu.SemaphoreType.DMA((5,)),
            pltpu.SemaphoreType.DMA((planes, 2)),
        ] + [sem] * 13,
        compiler_params=pltpu.CompilerParams(
            collective_id=0, has_side_effects=True, vmem_limit_bytes=60 * 1024 * 1024),
        cost_estimate=pl.CostEstimate(
            flops=4 * row_count * width * owners * local, transcendentals=row_count * 64,
            bytes_accessed=2 * row_count * width),
    )(embeddings, level_ids.reshape(1, -1), centroids, empty_ids.reshape(1, -1), reseed_rows.reshape(1, -1))
    return new_centroids, counts.reshape(-1)


def solution(mesh):
    in_specs = (
        P(("groups", "owners"), None),
        P(("groups", "owners")),
        P(("groups", "owners"), None),
        P("groups"),
        P("groups"),
    )
    out_specs = (P(("groups", "owners"), None), P(("groups", "owners")))
    return jax.shard_map(functools.partial(shards, mesh.shape["owners"]), mesh=mesh,
                         in_specs=in_specs, out_specs=out_specs, check_vma=False)
```
